32 devices in a mesh: row: 8 (over y, x, core), col: 4 (over z).
Axes of the slice: x: 2, y: 2, z: 4, core: 2. Of those that a mesh axis runs over, the one named last changes fastest.
Arguments:
- halves: bfloat16 [24, 800, 800], P(None, 'row', 'col'), may hold values from -6 to 6
- first_factor: bfloat16 [4000, 800], P('col'), may hold values from -0.21875 to 0.21875
- second_factor: bfloat16 [4000, 800], P('col'), may hold values from -0.09375 to 0.09375
- weights: bfloat16 [4000, 24], P('col'), may hold values from 0.25 to 4
Outputs:
- cycle: bfloat16 [24, 800, 800], P('col', 'row')
The draws below stay inside these ranges and needn't reach their ends.
All inputs are finite; a program needn't handle non-finite values.
Results may differ from the reference program's by a relative error of at most 0.0095.
Values may be sent and summed in bfloat16 or wider, within the bound.
A program may use at most 64 MiB of HBM per device.

```python
import math
import jax
import jax.numpy as jnp
from jax import lax

V = 800
NQ = 4000
O = 24
QB = 1000


def steps_of(rng, shape, pieces, smallest, high):
    def one(dim, parts):
        heights = jax.random.uniform(jax.random.fold_in(jax.random.fold_in(rng, 6), dim), (parts,), jnp.float32, smallest / len(pieces), high / len(pieces))
        return jnp.repeat(jnp.exp(heights), shape[dim] // parts).reshape((-1,) + (1,) * (len(shape) - dim - 1))

    loudness = one(*pieces[0])
    for cut in pieces[1:]:
        loudness = loudness * one(*cut)
    return loudness


def bell_draw(rng, dims, spread, limit, shards=(), held_as=jnp.bfloat16):
    drawn = spread * jax.random.normal(rng, dims, jnp.float32)
    if shards:
        drawn = drawn * steps_of(rng, dims, shards, -0.22, 0.18)
    return jnp.clip(drawn, -limit, limit).astype(held_as)


def setup_inputs(seed: int = 0) -> dict:
    seeds = jax.random.split(jax.random.key(seed), 5)
    return {
        "halves": bell_draw(seeds[0], (O, V, V), 1.0, 6.0, ((1, 8), (2, 4))),
        "first_factor": bell_draw(seeds[1], (NQ, V), V ** -0.5, 0.21875, ((0, 4),)),
        "second_factor": bell_draw(seeds[2], (NQ, V), NQ ** -0.5, 0.09375, ((0, 4),)),
        "weights": jnp.clip(jnp.exp(math.log(4.0) - 2.7725887 * jax.random.uniform(seeds[3], (NQ, O), jnp.float32) ** steps_of(seeds[3], (NQ, O), ((0, 4),), -0.2, 0.2)), 0.25, 4.0).astype(jnp.bfloat16),
    }


def reference(halves, first_factor, second_factor, weights):
    block_count = NQ // QB
    right_blocks = second_factor.reshape(block_count, QB, V).astype(jnp.float32)

    def one_orbital(index):
        sheet = lax.dynamic_index_in_dim(halves, index, 0, keepdims=False)
        amplitude = (sheet.astype(jnp.float32) - sheet.T.astype(jnp.float32)).astype(jnp.bfloat16)
        scale = lax.dynamic_index_in_dim(weights, index, 1, keepdims=False).astype(jnp.float32)
        scaled = (jnp.dot(amplitude, first_factor.T, preferred_element_type=jnp.float32) * scale[None, :]).astype(jnp.bfloat16)
        blocks = jnp.einsum("akq,kqc->kac", scaled.reshape(V, block_count, QB).astype(jnp.float32), right_blocks)
        blocks = lax.optimization_barrier(blocks.astype(jnp.bfloat16)).astype(jnp.float32)
        return jnp.sum(blocks, axis=0).astype(jnp.bfloat16)

    return lax.map(one_orbital, jnp.arange(O, dtype=jnp.int32))
```

```python
import jax
import jax.numpy as jnp
from jax import lax
from jax.sharding import PartitionSpec as P


def spread(block, rows):
    piece = -(-block.shape[0] // rows)
    pad = piece * rows - block.shape[0]
    if pad:
        block = jnp.pad(block, ((0, pad), (0, 0)))
    mine = lax.dynamic_slice_in_dim(block, lax.axis_index("row") * piece, piece, 0)
    everywhere = lax.all_gather(mine, "col", axis=0, tiled=False)
    return lax.all_gather(everywhere, "row", axis=0, tiled=False)


def body(rows, halves, first_factor, second_factor, weights):
    count = halves.shape[0] // lax.axis_size("col")
    first = spread(first_factor, rows)
    second = spread(second_factor, rows)
    scale = spread(weights, rows)
    first = first.reshape(-1, first.shape[-1])
    second = second.reshape(-1, second.shape[-1])
    scale = scale.reshape(-1, scale.shape[-1])
    scale = lax.dynamic_slice_in_dim(scale, lax.axis_index("col") * count, count, 1)
    regrouped = lax.all_to_all(halves, "col", split_axis=0, concat_axis=2, tiled=True)
    mirrored = lax.all_to_all(regrouped, "row", split_axis=2, concat_axis=1, tiled=True)
    amplitude = (
        regrouped.astype(jnp.float32) - jnp.swapaxes(mirrored, 1, 2).astype(jnp.float32)
    ).astype(jnp.bfloat16)
    scaled = jnp.einsum("iab,qb->iaq", amplitude, first, preferred_element_type=jnp.float32)
    scaled = (scaled * jnp.transpose(scale).astype(jnp.float32)[:, None, :]).astype(jnp.bfloat16)
    return jnp.einsum("iaq,qc->iac", scaled, second, preferred_element_type=jnp.float32).astype(
        jnp.bfloat16
    )


def solution(mesh):
    placed = (P(None, "row", "col"), P("col", None), P("col", None), P("col", None))
    rows = mesh.shape["row"]

    def run(*arrays):
        return body(rows, *arrays)

    return jax.shard_map(
        run, mesh=mesh, in_specs=placed, out_specs=P("col", "row", None), check_vma=False
    )
```

```python
import functools

import jax
import jax.numpy as jnp
from jax import lax
from jax.experimental import pallas as pl
from jax.experimental.pallas import tpu as pltpu
from jax.sharding import PartitionSpec as P


def spread(block, rows):
    piece = -(-block.shape[0] // rows)
    pad = piece * rows - block.shape[0]
    if pad:
        block = jnp.pad(block, ((0, pad), (0, 0)))
    mine = lax.dynamic_slice_in_dim(block, lax.axis_index("row") * piece, piece, 0)
    everywhere = lax.all_gather(mine, "col", axis=0, tiled=False)
    return lax.all_gather(everywhere, "row", axis=0, tiled=False)


def body(rows, halves, first_factor, second_factor, weights):
    count = halves.shape[0] // lax.axis_size("col")
    first = spread(first_factor, rows)
    second = spread(second_factor, rows)
    scale = spread(weights, rows)
    first = first.reshape(-1, first.shape[-1])
    second = second.reshape(-1, second.shape[-1])
    scale = scale.reshape(-1, scale.shape[-1])
    scale = lax.dynamic_slice_in_dim(scale, lax.axis_index("col") * count, count, 1)
    regrouped = lax.all_to_all(halves, "col", split_axis=0, concat_axis=2, tiled=True)
    mirrored = lax.all_to_all(regrouped, "row", split_axis=2, concat_axis=1, tiled=True)
    amplitude = (
        regrouped.astype(jnp.float32) - jnp.swapaxes(mirrored, 1, 2).astype(jnp.float32)
    ).astype(jnp.bfloat16)
    scaled = jnp.einsum("iab,qb->iaq", amplitude, first, preferred_element_type=jnp.float32)
    scaled = (scaled * jnp.transpose(scale).astype(jnp.float32)[:, None, :]).astype(jnp.bfloat16)
    return jnp.einsum("iaq,qc->iac", scaled, second, preferred_element_type=jnp.float32).astype(
        jnp.bfloat16
    )


def up(value, unit):
    return -(-value // unit) * unit


def kernel(R, Z, n, wide, L, fin, hin, out, F, X, Y, A, acc, ws, rs, rr,
           fz_s, fz_r, fp_s, fp_r, h_s, h_r, y_s, y_r, a_s, a_r, r_s, r_r, loc):
    f32, bf16 = jnp.float32, jnp.bfloat16
    S, C = R // Z, R // 2
    count, tall, lanes = X.shape[1:]
    K = A.shape[2]
    r, z = lax.axis_index("row"), lax.axis_index("col")
    p, core = r // 2, lax.rem(r, 2)
    mate = r + 1 - 2 * core

    def send(src, dst, ss, sr, row, col):
        return pltpu.make_async_remote_copy(
            src_ref=src, dst_ref=dst, send_sem=ss, recv_sem=sr,
            device_id={"row": row, "col": col}, device_id_type=pl.DeviceIdType.MESH)

    barrier = pltpu.get_barrier_semaphore()
    for d in range(1, R):
        pl.semaphore_signal(barrier, inc=1, device_id={"row": lax.rem(r + d, R), "col": z},
                            device_id_type=pl.DeviceIdType.MESH)
    for d in range(1, Z):
        pl.semaphore_signal(barrier, inc=1, device_id={"row": r, "col": lax.rem(z + d, Z)},
                            device_id_type=pl.DeviceIdType.MESH)
    pl.semaphore_wait(barrier, R + Z - 2)

    sent = []
    own = pltpu.make_async_copy(hin.at[pl.ds(z * S, S)], X.at[pl.ds(z * S, S)], loc)
    piece = pl.ds(pl.multiple_of(p * wide, 128), wide)
    hs, fs = [], []
    for d in range(1, Z):
        to = lax.rem(z + d, Z)
        hs.append(send(hin.at[pl.ds(to * S, S)], X.at[pl.ds(z * S, S)], h_s.at[d - 1], h_r.at[d - 1], r, to))
        fs.append(send(fin.at[:, piece], F.at[z, :, piece], fz_s.at[d - 1], fz_r.at[d - 1], r, to))
    for c in hs + fs:
        c.start()
    own.start()
    sent += hs + fs

    for c in hs:
        c.wait_recv()
    own.wait()
    ys = []
    for d in range(1, R):
        to = lax.rem(r + d, R)
        ys.append(send(X.at[to], Y.at[r], y_s.at[d - 1], y_r.at[d - 1], to, z))
        ys[-1].start()
    mine = pltpu.make_async_copy(X.at[r], Y.at[r], loc)
    mine.start()
    sent += ys
    fps = {}
    for d in range(1, Z):
        fs[d - 1].wait_recv()
        src = lax.rem(z + Z - d, Z)
        for e in range(1, C):
            to = lax.rem(p + e, C) * 2 + core
            c = send(F.at[src, :, piece], F.at[src, :, piece], fp_s.at[d - 1, e - 1], fp_r.at[d - 1, e - 1], to, z)
            c.start()
            fps[d, e] = c
            sent.append(c)
    for c in ys:
        c.wait_recv()
    mine.wait()

    @pl.loop(0, count)
    def _(i):
        tiles = [jnp.zeros((tall, lanes), f32) for _ in range(K // 128)]
        for j in range(R):
            y = jnp.concatenate([Y[j, i].astype(f32), jnp.zeros((lanes - tall, lanes), f32)], axis=0)
            v = X[j, i].astype(f32) - jnp.transpose(y)[:tall]
            q, rem = divmod(j * tall, 128)
            if rem + tall <= 128:
                tiles[q] += pltpu.roll(v, rem, 1) if rem else v
            else:
                w = pltpu.roll(v, rem, 1)
                at = lax.broadcasted_iota(jnp.int32, (tall, lanes), 1)
                tiles[q] += jnp.where(at >= rem, w, 0.0)
                tiles[q + 1] += jnp.where(at < rem, w, 0.0)
        start = pl.multiple_of(i * tall, 16)
        for q in range(K // 128):
            A[0, pl.ds(start, tall), pl.ds(q * 128, 128)] = tiles[q].astype(bf16)

    swap = send(A.at[0], A.at[1], a_s, a_r, mate, z)
    swap.start()
    sent.append(swap)

    half = count // 2 if count % 2 == 0 else count
    top = K + n

    def compute(block, slot, first):
        @pl.loop(0, count // half)
        def _(c):
            rows = pl.ds(pl.multiple_of(c * half * tall, 16), half * tall)
            t = jnp.dot(A[slot, rows, :], block[0:K, :], preferred_element_type=f32)
            t = jnp.concatenate(
                [t[g * tall:(g + 1) * tall] * ws[pl.ds(c * half + g, 1), :] for g in range(half)], axis=0
            ).astype(bf16)
            o = lax.dot_general(t, block[K:top, :], (((1,), (1,)), ((), ())), preferred_element_type=f32)
            if first:
                acc[slot, rows, :] = o
            else:
                acc[slot, rows, :] += o

    back = send(rs, rr, r_s, r_r, mate, z)
    sent.append(back)
    for d in range(Z):
        if d:
            for e in range(1, C):
                fps[d, e].wait_recv()
            block = F.at[lax.rem(z + Z - d, Z)]
        else:
            block = fin
        shape = (ws.shape[0], L - top)
        pick = lax.broadcasted_iota(jnp.int32, shape, 1) == lax.broadcasted_iota(jnp.int32, shape, 0) + z * count
        ws[...] = jnp.dot(jnp.where(pick, 1.0, 0.0).astype(bf16), block[top:L, :], preferred_element_type=f32)
        if d == 0:
            compute(block, 0, True)
            swap.wait_recv()
            compute(block, 1, True)
        else:
            compute(block, 1, False)
            if d == Z - 1:
                rs[...] = acc[1].astype(bf16)
                back.start()
            compute(block, 0, False)
    back.wait_recv()
    for i in range(count):
        rows = slice(i * tall, (i + 1) * tall)
        out[i] = (acc[0, rows, :] + rr[rows, :].astype(f32)).astype(bf16)[: out.shape[1]]
    for c in sent:
        c.wait_send()


def fused(R, Z, halves, first_factor, second_factor, weights):
    bf16 = jnp.bfloat16
    S, C = R // Z, R // 2
    O, a, b = halves.shape
    q, v = first_factor.shape
    n = second_factor.shape[1]
    count, step = O // Z, b // S
    tall, lanes = up(a, 16), 128
    K = up(R * tall, 128)
    wide = up(-(-q // R), 128)
    core = lax.rem(lax.axis_index("row"), 2)
    one = first_factor.T.reshape(R, a, q)
    one = jnp.pad(one, ((0, 0), (0, tall - a), (0, 0))).reshape(R * tall, q)
    w = weights.T
    L = up(K + n + O, 16)
    full = jnp.concatenate([jnp.pad(one, ((0, K - R * tall), (0, 0))), second_factor.T, w], axis=0)
    full = jnp.pad(full, ((0, L - K - n - O), (0, R * wide - q)))
    fin = lax.dynamic_slice_in_dim(full, core * (C * wide), C * wide, 1)
    hin = halves.reshape(Z, count, a, S, step).transpose(0, 3, 1, 2, 4).reshape(R, count, a, step)
    hin = jnp.pad(hin, ((0, 0), (0, 0), (0, tall - a), (0, lanes - step)))
    dma, vmem = pltpu.SemaphoreType.DMA, pltpu.VMEM
    big = pl.BlockSpec(memory_space=pltpu.VMEM)
    return pl.pallas_call(
        functools.partial(kernel, R, Z, n, wide, L),
        out_shape=jax.ShapeDtypeStruct((count, a, n), bf16),
        in_specs=[big, big],
        out_specs=big,
        scratch_shapes=[
            vmem((Z, L, C * wide), bf16),
            vmem((R, count, tall, lanes), bf16),
            vmem((R, count, tall, lanes), bf16),
            vmem((2, count * tall, K), bf16),
            vmem((2, count * tall, n), jnp.float32),
            vmem((up(count, 16), C * wide), jnp.float32),
            vmem((count * tall, n), bf16),
            vmem((count * tall, n), bf16),
            dma((Z - 1,)), dma((Z - 1,)),
            dma((Z - 1, C - 1)), dma((Z - 1, C - 1)),
            dma((Z - 1,)), dma((Z - 1,)),
            dma((R - 1,)), dma((R - 1,)),
            dma, dma, dma, dma, dma,
        ],
        compiler_params=pltpu.CompilerParams(
            collective_id=0, has_side_effects=True, vmem_limit_bytes=56 * 1024 * 1024
        ),
    )(fin, hin)


def fits(mesh):
    R, Z = mesh.shape["row"], mesh.shape["col"]
    return R % Z == 0 and R % 2 == 0 and R <= 8


def solution(mesh):
    placed = (P(None, "row", "col"), P("col", None), P("col", None), P("col", None))
    rows, cols = mesh.shape["row"], mesh.shape["col"]

    def run(*arrays):
        if fits(mesh):
            return fused(rows, cols, *arrays)
        return body(rows, *arrays)

    return jax.shard_map(
        run, mesh=mesh, in_specs=placed, out_specs=P("col", "row", None), check_vma=False
    )
```

```python
import functools

import jax
import jax.numpy as jnp
from jax import lax
from jax.experimental import pallas as pl
from jax.experimental.pallas import tpu as pltpu
from jax.sharding import PartitionSpec as P


def spread(block, rows):
    piece = -(-block.shape[0] // rows)
    pad = piece * rows - block.shape[0]
    if pad:
        block = jnp.pad(block, ((0, pad), (0, 0)))
    mine = lax.dynamic_slice_in_dim(block, lax.axis_index("row") * piece, piece, 0)
    everywhere = lax.all_gather(mine, "col", axis=0, tiled=False)
    return lax.all_gather(everywhere, "row", axis=0, tiled=False)


def body(rows, halves, first_factor, second_factor, weights):
    count = halves.shape[0] // lax.axis_size("col")
    first = spread(first_factor, rows)
    second = spread(second_factor, rows)
    scale = spread(weights, rows)
    first = first.reshape(-1, first.shape[-1])
    second = second.reshape(-1, second.shape[-1])
    scale = scale.reshape(-1, scale.shape[-1])
    scale = lax.dynamic_slice_in_dim(scale, lax.axis_index("col") * count, count, 1)
    regrouped = lax.all_to_all(halves, "col", split_axis=0, concat_axis=2, tiled=True)
    mirrored = lax.all_to_all(regrouped, "row", split_axis=2, concat_axis=1, tiled=True)
    amplitude = (
        regrouped.astype(jnp.float32) - jnp.swapaxes(mirrored, 1, 2).astype(jnp.float32)
    ).astype(jnp.bfloat16)
    scaled = jnp.einsum("iab,qb->iaq", amplitude, first, preferred_element_type=jnp.float32)
    scaled = (scaled * jnp.transpose(scale).astype(jnp.float32)[:, None, :]).astype(jnp.bfloat16)
    return jnp.einsum("iaq,qc->iac", scaled, second, preferred_element_type=jnp.float32).astype(
        jnp.bfloat16
    )


def up(value, unit):
    return -(-value // unit) * unit


def kernel(R, Z, n, wide, L, fin, hin, out, F, X, Y, A, acc, ws, rs, rr,
           fz_s, fz_r, fp_s, fp_r, fd_s, fd_r, h_s, h_r, y_s, y_r, a_s, a_r, r_s, r_r, loc):
    f32, bf16 = jnp.float32, jnp.bfloat16
    S, C = R // Z, R // 2
    count, tall, lanes = X.shape[1:]
    size = out.shape[1]
    K = A.shape[2]
    r, z = lax.axis_index("row"), lax.axis_index("col")
    p, core = r // 2, lax.rem(r, 2)
    mate = r + 1 - 2 * core

    def send(src, dst, ss, sr, row, col):
        return pltpu.make_async_remote_copy(
            src_ref=src, dst_ref=dst, send_sem=ss, recv_sem=sr,
            device_id={"row": row, "col": col}, device_id_type=pl.DeviceIdType.MESH)

    barrier = pltpu.get_barrier_semaphore()
    for d in range(1, R):
        pl.semaphore_signal(barrier, inc=1, device_id={"row": lax.rem(r + d, R), "col": z},
                            device_id_type=pl.DeviceIdType.MESH)
    for d in range(1, Z):
        pl.semaphore_signal(barrier, inc=1, device_id={"row": r, "col": lax.rem(z + d, Z)},
                            device_id_type=pl.DeviceIdType.MESH)
    pl.semaphore_wait(barrier, R + Z - 2)

    sent = []
    own = pltpu.make_async_copy(hin.at[pl.ds(z * S, S)], X.at[pl.ds(z * S, S)], loc)
    px, py = p + 1 - 2 * lax.rem(p, 2), lax.rem(p + 2, C)

    def lane(q):
        return pl.ds(pl.multiple_of(q * wide, 128), wide)

    def along(side, step, src, src_ref):
        return send(src_ref, F.at[src, :, lane(p)], fz_s.at[side, step - 1], fz_r.at[side, step - 1],
                    r, z + 1 - 2 * side)

    firsts = [along(side, 1, z, fin.at[:, lane(p)]) for side in range(2)]
    can = [z + 1 < Z, z > 0]
    for side in range(2):
        pl.when(can[side])(firsts[side].start)
    hs = []
    for d in range(1, Z):
        to = lax.rem(z + d, Z)
        hs.append(send(hin.at[pl.ds(to * S, S)], X.at[pl.ds(z * S, S)], h_s.at[d - 1], h_r.at[d - 1], r, to))
        hs[-1].start()
    own.start()
    sent += hs

    near = jnp.minimum(z, Z - 1 - z)
    longer = jnp.where(z > Z - 1 - z, 0, 1)
    blocks = []
    cut = L // 32 * 16
    for k in range(1, Z):
        paired = k <= 2 * near
        step = jnp.where(paired, (k + 1) // 2, k - near)
        side = jnp.where(paired, (k - 1) % 2, longer)
        src = z + step * (2 * side - 1)
        come = along(side, step, src, F.at[src, :, lane(p)])
        go = along(side, step + 1, src, F.at[src, :, lane(p)])
        on = jnp.where(side == 0, z + 1 < Z, z > 0)
        mine = F.at[src, :, lane(p)]
        plane = [send(mine, mine, fp_s.at[k - 1, g], fp_r.at[k - 1, g], to * 2 + core, z)
                 for g, to in enumerate((px, py))]
        high = F.at[src, pl.ds(0, cut), lane(px)]
        low = F.at[src, pl.ds(cut, L - cut), lane(py)]
        corner = [send(high, high, fd_s.at[k - 1, 0], fd_r.at[k - 1, 0], py * 2 + core, z),
                  send(low, low, fd_s.at[k - 1, 1], fd_r.at[k - 1, 1], px * 2 + core, z)]
        blocks.append((src, come, go, on, plane, corner))
        sent += plane + corner

    def arrive(k):
        src, come, go, on, plane, corner = blocks[k - 1]
        come.wait_recv()
        pl.when(on)(go.start)
        for c in plane:
            c.start()

    def turn(k):
        plane, corner = blocks[k - 1][4:]
        for c, f in zip(plane, corner):
            c.wait_recv()
            f.start()

    arrive(1)
    for k in range(2, Z - 1):
        arrive(k)
    turn(1)
    for c in hs:
        c.wait_recv()
    own.wait()
    ys = []
    for d in range(1, R):
        to = lax.rem(r + d, R)
        ys.append(send(X.at[to], Y.at[r], y_s.at[d - 1], y_r.at[d - 1], to, z))
        ys[-1].start()
    mine = pltpu.make_async_copy(X.at[r], Y.at[r], loc)
    mine.start()
    sent += ys
    for k in range(2, Z - 1):
        turn(k)
    if Z > 2:
        arrive(Z - 1)
    for c in ys:
        c.wait_recv()
    mine.wait()

    @pl.loop(0, count)
    def _(i):
        tiles = [jnp.zeros((tall, lanes), f32) for _ in range(K // 128)]
        for j in range(R):
            y = jnp.concatenate([Y[j, i].astype(f32), jnp.zeros((lanes - tall, lanes), f32)], axis=0)
            v = X[j, i].astype(f32) - jnp.transpose(y)[:tall]
            q, rem = divmod(j * size, 128)
            if rem + size <= 128:
                tiles[q] += pltpu.roll(v, rem, 1) if rem else v
            else:
                w = pltpu.roll(v, rem, 1)
                at = lax.broadcasted_iota(jnp.int32, (tall, lanes), 1)
                tiles[q] += jnp.where(at >= rem, w, 0.0)
                tiles[q + 1] += jnp.where(at < rem, w, 0.0)
        start = pl.multiple_of(i * tall, 16)
        for q in range(K // 128):
            A[0, pl.ds(start, tall), pl.ds(q * 128, 128)] = tiles[q].astype(bf16)

    swap = send(A.at[0], A.at[1], a_s, a_r, mate, z)
    swap.start()
    sent.append(swap)

    half = count // 2 if count % 2 == 0 else count
    low, top = R * size, R * size + n

    def compute(block, slot, first):
        @pl.loop(0, count // half)
        def _(c):
            rows = pl.ds(pl.multiple_of(c * half * tall, 16), half * tall)
            t = jnp.dot(A[slot, rows, :], block[0:K, :], preferred_element_type=f32)
            t = jnp.concatenate(
                [t[g * tall:(g + 1) * tall] * ws[pl.ds(c * half + g, 1), :] for g in range(half)], axis=0
            ).astype(bf16)
            o = lax.dot_general(t, block[low:top, :], (((1,), (1,)), ((), ())), preferred_element_type=f32)
            if first:
                acc[slot, rows, :] = o
            else:
                acc[slot, rows, :] += o

    back = send(rs, rr, r_s, r_r, mate, z)
    sent.append(back)
    for k in range(Z):
        if k:
            for c in blocks[k - 1][5]:
                c.wait_recv()
            block = F.at[blocks[k - 1][0]]
        else:
            block = fin
        shape = (ws.shape[0], L - top)
        pick = lax.broadcasted_iota(jnp.int32, shape, 1) == lax.broadcasted_iota(jnp.int32, shape, 0) + z * count
        ws[...] = jnp.dot(jnp.where(pick, 1.0, 0.0).astype(bf16), block[top:L, :], preferred_element_type=f32)
        if k == 0:
            compute(block, 0, True)
            swap.wait_recv()
            compute(block, 1, True)
            if Z > 2:
                turn(Z - 1)
        else:
            compute(block, 1, False)
            if k == Z - 1:
                rs[...] = acc[1].astype(bf16)
                back.start()
            compute(block, 0, False)
    back.wait_recv()
    for i in range(count):
        rows = slice(i * tall, (i + 1) * tall)
        out[i] = (acc[0, rows, :] + rr[rows, :].astype(f32)).astype(bf16)[: out.shape[1]]
    for c in sent:
        c.wait_send()
    for side in range(2):
        pl.when(can[side])(firsts[side].wait_send)
    for block in blocks:
        pl.when(block[3])(block[2].wait_send)


def fused(R, Z, halves, first_factor, second_factor, weights):
    bf16 = jnp.bfloat16
    S, C = R // Z, R // 2
    O, a, b = halves.shape
    q, v = first_factor.shape
    n = second_factor.shape[1]
    count, step = O // Z, b // S
    tall, lanes = up(a, 16), 128
    K = up(R * a, 128)
    wide = up(-(-q // R), 128)
    core = lax.rem(lax.axis_index("row"), 2)
    L = up(R * a + n + O, 16)
    full = jnp.concatenate([first_factor.T, second_factor.T, weights.T], axis=0)
    full = jnp.pad(full, ((0, L - R * a - n - O), (0, R * wide - q)))
    fin = lax.dynamic_slice_in_dim(full, core * (C * wide), C * wide, 1)
    hin = halves.reshape(Z, count, a, S, step).transpose(0, 3, 1, 2, 4).reshape(R, count, a, step)
    hin = jnp.pad(hin, ((0, 0), (0, 0), (0, tall - a), (0, lanes - step)))
    dma, vmem = pltpu.SemaphoreType.DMA, pltpu.VMEM
    big = pl.BlockSpec(memory_space=pltpu.VMEM)
    return pl.pallas_call(
        functools.partial(kernel, R, Z, n, wide, L),
        out_shape=jax.ShapeDtypeStruct((count, a, n), bf16),
        in_specs=[big, big],
        out_specs=big,
        scratch_shapes=[
            vmem((Z, L, C * wide), bf16),
            vmem((R, count, tall, lanes), bf16),
            vmem((R, count, tall, lanes), bf16),
            vmem((2, count * tall, K), bf16),
            vmem((2, count * tall, n), jnp.float32),
            vmem((up(count, 16), C * wide), jnp.float32),
            vmem((count * tall, n), bf16),
            vmem((count * tall, n), bf16),
            dma((2, Z)), dma((2, Z)),
            dma((Z - 1, 2)), dma((Z - 1, 2)),
            dma((Z - 1, 2)), dma((Z - 1, 2)),
            dma((Z - 1,)), dma((Z - 1,)),
            dma((R - 1,)), dma((R - 1,)),
            dma, dma, dma, dma, dma,
        ],
        compiler_params=pltpu.CompilerParams(
            collective_id=0, has_side_effects=True, vmem_limit_bytes=56 * 1024 * 1024
        ),
    )(fin, hin)


def fits(mesh):
    R, Z = mesh.shape["row"], mesh.shape["col"]
    return R % Z == 0 and R == 8 and Z > 2


def solution(mesh):
    placed = (P(None, "row", "col"), P("col", None), P("col", None), P("col", None))
    rows, cols = mesh.shape["row"], mesh.shape["col"]

    def run(*arrays):
        if fits(mesh):
            return fused(rows, cols, *arrays)
        return body(rows, *arrays)

    return jax.shard_map(
        run, mesh=mesh, in_specs=placed, out_specs=P("col", "row", None), check_vma=False
    )
```

```python
import functools

import jax
import jax.numpy as jnp
from jax import lax
from jax.experimental import pallas as pl
from jax.experimental.pallas import tpu as pltpu
from jax.sharding import PartitionSpec as P


def spread(block, rows):
    piece = -(-block.shape[0] // rows)
    pad = piece * rows - block.shape[0]
    if pad:
        block = jnp.pad(block, ((0, pad), (0, 0)))
    mine = lax.dynamic_slice_in_dim(block, lax.axis_index("row") * piece, piece, 0)
    everywhere = lax.all_gather(mine, "col", axis=0, tiled=False)
    return lax.all_gather(everywhere, "row", axis=0, tiled=False)


def body(rows, halves, first_factor, second_factor, weights):
    count = halves.shape[0] // lax.axis_size("col")
    first = spread(first_factor, rows)
    second = spread(second_factor, rows)
    scale = spread(weights, rows)
    first = first.reshape(-1, first.shape[-1])
    second = second.reshape(-1, second.shape[-1])
    scale = scale.reshape(-1, scale.shape[-1])
    scale = lax.dynamic_slice_in_dim(scale, lax.axis_index("col") * count, count, 1)
    regrouped = lax.all_to_all(halves, "col", split_axis=0, concat_axis=2, tiled=True)
    mirrored = lax.all_to_all(regrouped, "row", split_axis=2, concat_axis=1, tiled=True)
    amplitude = (
        regrouped.astype(jnp.float32) - jnp.swapaxes(mirrored, 1, 2).astype(jnp.float32)
    ).astype(jnp.bfloat16)
    scaled = jnp.einsum("iab,qb->iaq", amplitude, first, preferred_element_type=jnp.float32)
    scaled = (scaled * jnp.transpose(scale).astype(jnp.float32)[:, None, :]).astype(jnp.bfloat16)
    return jnp.einsum("iaq,qc->iac", scaled, second, preferred_element_type=jnp.float32).astype(
        jnp.bfloat16
    )


def up(value, unit):
    return -(-value // unit) * unit


def kernel(R, Z, n, wide, L, fin, hin, out, F, X, Y, A, acc, ws, rs, rr,
           fz_s, fz_r, fp_s, fp_r, fd_s, fd_r, h_s, h_r, y_s, y_r, a_s, a_r, r_s, r_r, loc):
    f32, bf16 = jnp.float32, jnp.bfloat16
    S, C = R // Z, R // 2
    tall = X.shape[1]
    count, size = out.shape[:2]
    lanes = 128
    K = A.shape[2]
    r, z = lax.axis_index("row"), lax.axis_index("col")
    p, core = r // 2, lax.rem(r, 2)
    mate = r + 1 - 2 * core

    def send(src, dst, ss, sr, row, col):
        return pltpu.make_async_remote_copy(
            src_ref=src, dst_ref=dst, send_sem=ss, recv_sem=sr,
            device_id={"row": row, "col": col}, device_id_type=pl.DeviceIdType.MESH)

    barrier = pltpu.get_barrier_semaphore()
    for d in range(1, R):
        pl.semaphore_signal(barrier, inc=1, device_id={"row": lax.rem(r + d, R), "col": z},
                            device_id_type=pl.DeviceIdType.MESH)
    for d in range(1, Z):
        pl.semaphore_signal(barrier, inc=1, device_id={"row": r, "col": lax.rem(z + d, Z)},
                            device_id_type=pl.DeviceIdType.MESH)
    pl.semaphore_wait(barrier, R + Z - 2)

    sent = []
    own = pltpu.make_async_copy(hin.at[pl.ds(z * S, S)], X.at[pl.ds(z * S, S)], loc)
    px, py = p + 1 - 2 * lax.rem(p, 2), lax.rem(p + 2, C)

    def lane(q):
        return pl.ds(pl.multiple_of(q * wide, 128), wide)

    cut = L // 32 * 16
    parts = (pl.ds(0, cut), pl.ds(cut, L - cut))

    def along(side, step, src, h, src_ref):
        return send(src_ref, F.at[src, parts[h], lane(p)], fz_s.at[side, step - 1, h],
                    fz_r.at[side, step - 1, h], r, z + 1 - 2 * side)

    can = [z + 1 < Z, z > 0]
    firsts = []
    for h in range(2):
        for side in range(2):
            firsts.append((can[side], along(side, 1, z, h, fin.at[parts[h], lane(p)])))
            pl.when(can[side])(firsts[-1][1].start)
    hs = []
    for d in range(1, Z):
        to = lax.rem(z + d, Z)
        hs.append(send(hin.at[pl.ds(to * S, S)], X.at[pl.ds(z * S, S)], h_s.at[d - 1], h_r.at[d - 1], r, to))
        hs[-1].start()
    own.start()
    sent += hs

    near = jnp.minimum(z, Z - 1 - z)
    longer = jnp.where(z > Z - 1 - z, 0, 1)
    blocks = []
    for k in range(1, Z):
        paired = k <= 2 * near
        step = jnp.where(paired, (k + 1) // 2, k - near)
        side = jnp.where(paired, (k - 1) % 2, longer)
        src = z + step * (2 * side - 1)
        on = jnp.where(side == 0, z + 1 < Z, z > 0)
        come, go, plane = [], [], []
        for h in range(2):
            mine = F.at[src, parts[h], lane(p)]
            come.append(along(side, step, src, h, mine))
            go.append(along(side, step + 1, src, h, mine))
            plane.append([send(mine, mine, fp_s.at[k - 1, h, g], fp_r.at[k - 1, h, g], to * 2 + core, z)
                          for g, to in enumerate((px, py))])
        high = F.at[src, parts[0], lane(px)]
        low = F.at[src, parts[1], lane(py)]
        corner = [send(high, high, fd_s.at[k - 1, 0], fd_r.at[k - 1, 0], py * 2 + core, z),
                  send(low, low, fd_s.at[k - 1, 1], fd_r.at[k - 1, 1], px * 2 + core, z)]
        blocks.append((src, come, go, on, plane, corner))
        sent += plane[0] + plane[1] + corner

    def arrive(k):
        src, come, go, on, plane, corner = blocks[k - 1]
        for h in range(2):
            come[h].wait_recv()
            pl.when(on)(go[h].start)
            plane[h][h].start()
            plane[h][1 - h].start()

    def turn(k):
        plane, corner = blocks[k - 1][4:]
        for h in range(2):
            plane[h][h].wait_recv()
            corner[h].start()

    arrive(1)
    for k in range(2, Z - 1):
        arrive(k)
    turn(1)
    for c in hs:
        c.wait_recv()
    own.wait()
    ys = []
    for d in range(1, R):
        to = lax.rem(r + d, R)
        ys.append(send(X.at[to], Y.at[r], y_s.at[d - 1], y_r.at[d - 1], to, z))
        ys[-1].start()
    mine = pltpu.make_async_copy(X.at[r], Y.at[r], loc)
    mine.start()
    sent += ys
    for k in range(2, Z - 1):
        turn(k)
    if Z > 2:
        arrive(Z - 1)
    for c in ys:
        c.wait_recv()
    mine.wait()

    at = lax.broadcasted_iota(jnp.int32, (tall, lanes), 1)

    def take(ref, j, i):
        q, rem = divmod(i * size, lanes)
        v = ref[j, :, q * lanes:(q + 1) * lanes].astype(f32)
        if rem:
            v = pltpu.roll(v, lanes - rem, 1)
        if rem + size > lanes:
            more = ref[j, :, (q + 1) * lanes:(q + 2) * lanes].astype(f32)
            v = jnp.where(at < lanes - rem, v, pltpu.roll(more, lanes - rem, 1))
        return jnp.where(at < size, v, 0.0)

    for i in range(count):
        tiles = [jnp.zeros((tall, lanes), f32) for _ in range(K // 128)]
        for j in range(R):
            y = jnp.concatenate([take(Y, j, i), jnp.zeros((lanes - tall, lanes), f32)], axis=0)
            v = take(X, j, i) - jnp.transpose(y)[:tall]
            q, rem = divmod(j * size, 128)
            if rem + size <= 128:
                tiles[q] += pltpu.roll(v, rem, 1) if rem else v
            else:
                w = pltpu.roll(v, rem, 1)
                tiles[q] += jnp.where(at >= rem, w, 0.0)
                tiles[q + 1] += jnp.where(at < rem, w, 0.0)
        start = i * tall
        for q in range(K // 128):
            A[0, pl.ds(start, tall), pl.ds(q * 128, 128)] = tiles[q].astype(bf16)

    swap = send(A.at[0], A.at[1], a_s, a_r, mate, z)
    swap.start()
    sent.append(swap)

    half = count // 2 if count % 2 == 0 else count
    low, top = R * size, R * size + n

    def compute(block, slot, first):
        @pl.loop(0, count // half)
        def _(c):
            rows = pl.ds(pl.multiple_of(c * half * tall, 16), half * tall)
            t = jnp.dot(A[slot, rows, :], block[0:K, :], preferred_element_type=f32)
            t = jnp.concatenate(
                [t[g * tall:(g + 1) * tall] * ws[pl.ds(c * half + g, 1), :] for g in range(half)], axis=0
            ).astype(bf16)
            o = lax.dot_general(t, block[low:top, :], (((1,), (1,)), ((), ())), preferred_element_type=f32)
            if first:
                acc[slot, rows, :] = o
            else:
                acc[slot, rows, :] += o

    back = send(rs, rr, r_s, r_r, mate, z)
    sent.append(back)
    for k in range(Z):
        if k:
            for c in blocks[k - 1][5] + [blocks[k - 1][4][0][1], blocks[k - 1][4][1][0]]:
                c.wait_recv()
            block = F.at[blocks[k - 1][0]]
        else:
            block = fin
        shape = (ws.shape[0], L - top)
        pick = lax.broadcasted_iota(jnp.int32, shape, 1) == lax.broadcasted_iota(jnp.int32, shape, 0) + z * count
        ws[...] = jnp.dot(jnp.where(pick, 1.0, 0.0).astype(bf16), block[top:L, :], preferred_element_type=f32)
        if k == 0:
            compute(block, 0, True)
            swap.wait_recv()
            compute(block, 1, True)
            if Z > 2:
                turn(Z - 1)
        else:
            compute(block, 1, False)
            if k == Z - 1:
                rs[...] = acc[1].astype(bf16)
                back.start()
            compute(block, 0, False)
    back.wait_recv()
    for i in range(count):
        rows = slice(i * tall, (i + 1) * tall)
        out[i] = (acc[0, rows, :] + rr[rows, :].astype(f32)).astype(bf16)[: out.shape[1]]
    for c in sent:
        c.wait_send()
    for there, c in firsts:
        pl.when(there)(c.wait_send)
    for block in blocks:
        for c in block[2]:
            pl.when(block[3])(c.wait_send)


def fused(R, Z, halves, first_factor, second_factor, weights):
    bf16 = jnp.bfloat16
    S, C = R // Z, R // 2
    O, a, b = halves.shape
    q, v = first_factor.shape
    n = second_factor.shape[1]
    count, step = O // Z, b // S
    tall = up(a, 16)
    K = up(R * a, 128)
    wide = up(-(-q // R), 128)
    core = lax.rem(lax.axis_index("row"), 2)
    L = up(R * a + n + O, 16)
    full = jnp.concatenate([first_factor.T, second_factor.T, weights.T], axis=0)
    full = jnp.pad(full, ((0, L - R * a - n - O), (0, R * wide - q)))
    fin = lax.dynamic_slice_in_dim(full, core * (C * wide), C * wide, 1)
    hin = halves.reshape(Z, count, a, S, step).transpose(0, 3, 2, 1, 4).reshape(R, a, count * step)
    lanes = up(count * step, 128)
    hin = jnp.pad(hin, ((0, 0), (0, tall - a), (0, lanes - count * step)))
    dma, vmem = pltpu.SemaphoreType.DMA, pltpu.VMEM
    big = pl.BlockSpec(memory_space=pltpu.VMEM)
    return pl.pallas_call(
        functools.partial(kernel, R, Z, n, wide, L),
        out_shape=jax.ShapeDtypeStruct((count, a, n), bf16),
        in_specs=[big, big],
        out_specs=big,
        scratch_shapes=[
            vmem((Z, L, C * wide), bf16),
            vmem((R, tall, lanes), bf16),
            vmem((R, tall, lanes), bf16),
            vmem((2, count * tall, K), bf16),
            vmem((2, count * tall, n), jnp.float32),
            vmem((up(count, 16), C * wide), jnp.float32),
            vmem((count * tall, n), bf16),
            vmem((count * tall, n), bf16),
            dma((2, Z, 2)), dma((2, Z, 2)),
            dma((Z - 1, 2, 2)), dma((Z - 1, 2, 2)),
            dma((Z - 1, 2)), dma((Z - 1, 2)),
            dma((Z - 1,)), dma((Z - 1,)),
            dma((R - 1,)), dma((R - 1,)),
            dma, dma, dma, dma, dma,
        ],
        compiler_params=pltpu.CompilerParams(
            collective_id=0, has_side_effects=True, vmem_limit_bytes=56 * 1024 * 1024
        ),
    )(fin, hin)


def fits(mesh):
    R, Z = mesh.shape["row"], mesh.shape["col"]
    return R % Z == 0 and R == 8 and Z > 2


def solution(mesh):
    placed = (P(None, "row", "col"), P("col", None), P("col", None), P("col", None))
    rows, cols = mesh.shape["row"], mesh.shape["col"]

    def run(*arrays):
        if fits(mesh):
            return fused(rows, cols, *arrays)
        return body(rows, *arrays)

    return jax.shard_map(
        run, mesh=mesh, in_specs=placed, out_specs=P("col", "row", None), check_vma=False
    )
```

```python
import functools

import jax
import jax.numpy as jnp
from jax import lax
from jax.experimental import pallas as pl
from jax.experimental.pallas import tpu as pltpu
from jax.sharding import PartitionSpec as P


def spread(block, rows):
    piece = -(-block.shape[0] // rows)
    pad = piece * rows - block.shape[0]
    if pad:
        block = jnp.pad(block, ((0, pad), (0, 0)))
    mine = lax.dynamic_slice_in_dim(block, lax.axis_index("row") * piece, piece, 0)
    everywhere = lax.all_gather(mine, "col", axis=0, tiled=False)
    return lax.all_gather(everywhere, "row", axis=0, tiled=False)


def body(rows, halves, first_factor, second_factor, weights):
    count = halves.shape[0] // lax.axis_size("col")
    first = spread(first_factor, rows)
    second = spread(second_factor, rows)
    scale = spread(weights, rows)
    first = first.reshape(-1, first.shape[-1])
    second = second.reshape(-1, second.shape[-1])
    scale = scale.reshape(-1, scale.shape[-1])
    scale = lax.dynamic_slice_in_dim(scale, lax.axis_index("col") * count, count, 1)
    regrouped = lax.all_to_all(halves, "col", split_axis=0, concat_axis=2, tiled=True)
    mirrored = lax.all_to_all(regrouped, "row", split_axis=2, concat_axis=1, tiled=True)
    amplitude = (
        regrouped.astype(jnp.float32) - jnp.swapaxes(mirrored, 1, 2).astype(jnp.float32)
    ).astype(jnp.bfloat16)
    scaled = jnp.einsum("iab,qb->iaq", amplitude, first, preferred_element_type=jnp.float32)
    scaled = (scaled * jnp.transpose(scale).astype(jnp.float32)[:, None, :]).astype(jnp.bfloat16)
    return jnp.einsum("iaq,qc->iac", scaled, second, preferred_element_type=jnp.float32).astype(
        jnp.bfloat16
    )


def up(value, unit):
    return -(-value // unit) * unit


def kernel(R, Z, n, wide, L, fin, hin, out, F, X, Y, A, acc, ws, rs, rr,
           fz_s, fz_r, fp_s, fp_r, fd_s, fd_r, h_s, h_r, y_s, y_r, a_s, a_r, r_s, r_r, loc):
    f32, bf16 = jnp.float32, jnp.bfloat16
    S, C = R // Z, R // 2
    tall = X.shape[1]
    count, size = out.shape[:2]
    lanes = 128
    K = A.shape[2]
    r, z = lax.axis_index("row"), lax.axis_index("col")
    p, core = r // 2, lax.rem(r, 2)
    mate = r + 1 - 2 * core

    def send(src, dst, ss, sr, row, col):
        return pltpu.make_async_remote_copy(
            src_ref=src, dst_ref=dst, send_sem=ss, recv_sem=sr,
            device_id={"row": row, "col": col}, device_id_type=pl.DeviceIdType.MESH)

    barrier = pltpu.get_barrier_semaphore()
    for d in range(1, R):
        pl.semaphore_signal(barrier, inc=1, device_id={"row": lax.rem(r + d, R), "col": z},
                            device_id_type=pl.DeviceIdType.MESH)
    for d in range(1, Z):
        pl.semaphore_signal(barrier, inc=1, device_id={"row": r, "col": lax.rem(z + d, Z)},
                            device_id_type=pl.DeviceIdType.MESH)
    pl.semaphore_wait(barrier, R + Z - 2)

    sent = []
    own = pltpu.make_async_copy(hin.at[pl.ds(z * S, S)], X.at[pl.ds(z * S, S)], loc)
    px, py = p + 1 - 2 * lax.rem(p, 2), lax.rem(p + 2, C)

    def lane(q):
        return pl.ds(pl.multiple_of(q * wide, 128), wide)

    cut = L // 32 * 16
    parts = (pl.ds(0, cut), pl.ds(cut, L - cut))

    def along(side, step, src, h, src_ref):
        return send(src_ref, F.at[src, parts[h], lane(p)], fz_s.at[side, step - 1, h],
                    fz_r.at[side, step - 1, h], r, z + 1 - 2 * side)

    can = [z + 1 < Z, z > 0]
    firsts = []
    for h in range(2):
        for side in range(2):
            firsts.append((can[side], along(side, 1, z, h, fin.at[parts[h], lane(p)])))
            pl.when(can[side])(firsts[-1][1].start)
    hs = []
    for d in range(1, Z):
        to = lax.rem(z + d, Z)
        hs.append(send(hin.at[pl.ds(to * S, S)], X.at[pl.ds(z * S, S)], h_s.at[d - 1], h_r.at[d - 1], r, to))
        hs[-1].start()
    own.start()
    sent += hs

    near = jnp.minimum(z, Z - 1 - z)
    longer = jnp.where(z > Z - 1 - z, 0, 1)
    blocks = []
    for k in range(1, Z):
        paired = k <= 2 * near
        step = jnp.where(paired, (k + 1) // 2, k - near)
        side = jnp.where(paired, (k - 1) % 2, longer)
        src = z + step * (2 * side - 1)
        on = jnp.where(side == 0, z + 1 < Z, z > 0)
        come, go, plane = [], [], []
        for h in range(2):
            mine = F.at[src, parts[h], lane(p)]
            come.append(along(side, step, src, h, mine))
            go.append(along(side, step + 1, src, h, mine))
            plane.append([send(mine, mine, fp_s.at[k - 1, h, g], fp_r.at[k - 1, h, g], to * 2 + core, z)
                          for g, to in enumerate((px, py))])
        high = F.at[src, parts[0], lane(px)]
        low = F.at[src, parts[1], lane(py)]
        corner = [send(high, high, fd_s.at[k - 1, 0], fd_r.at[k - 1, 0], py * 2 + core, z),
                  send(low, low, fd_s.at[k - 1, 1], fd_r.at[k - 1, 1], px * 2 + core, z)]
        blocks.append((src, come, go, on, plane, corner))
        sent += plane[0] + plane[1] + corner

    def arrive(k):
        src, come, go, on, plane, corner = blocks[k - 1]
        for h in range(2):
            come[h].wait_recv()
            pl.when(on)(go[h].start)
            plane[h][h].start()
            plane[h][1 - h].start()

    def turn(k):
        plane, corner = blocks[k - 1][4:]
        for h in range(2):
            plane[h][h].wait_recv()
            corner[h].start()

    arrive(1)
    turn(1)
    for k in range(2, Z - 1):
        arrive(k)
    for c in hs:
        c.wait_recv()
    own.wait()
    ys = []
    for d in range(1, R):
        to = lax.rem(r + d, R)
        ys.append(send(X.at[to], Y.at[r], y_s.at[d - 1], y_r.at[d - 1], to, z))
        ys[-1].start()
    mine = pltpu.make_async_copy(X.at[r], Y.at[r], loc)
    mine.start()
    sent += ys
    for k in range(2, Z - 1):
        turn(k)
    if Z > 2:
        arrive(Z - 1)
    for c in ys:
        c.wait_recv()
    mine.wait()

    at = lax.broadcasted_iota(jnp.int32, (tall, lanes), 1)

    def take(ref, j, i):
        q, rem = divmod(i * size, lanes)
        v = ref[j, :, q * lanes:(q + 1) * lanes].astype(f32)
        if rem:
            v = pltpu.roll(v, lanes - rem, 1)
        if rem + size > lanes:
            more = ref[j, :, (q + 1) * lanes:(q + 2) * lanes].astype(f32)
            v = jnp.where(at < lanes - rem, v, pltpu.roll(more, lanes - rem, 1))
        return jnp.where(at < size, v, 0.0)

    for i in range(count):
        tiles = [jnp.zeros((tall, lanes), f32) for _ in range(K // 128)]
        for j in range(R):
            y = jnp.concatenate([take(Y, j, i), jnp.zeros((lanes - tall, lanes), f32)], axis=0)
            v = take(X, j, i) - jnp.transpose(y)[:tall]
            q, rem = divmod(j * size, 128)
            if rem + size <= 128:
                tiles[q] += pltpu.roll(v, rem, 1) if rem else v
            else:
                w = pltpu.roll(v, rem, 1)
                tiles[q] += jnp.where(at >= rem, w, 0.0)
                tiles[q + 1] += jnp.where(at < rem, w, 0.0)
        start = i * tall
        for q in range(K // 128):
            A[0, pl.ds(start, tall), pl.ds(q * 128, 128)] = tiles[q].astype(bf16)

    swap = send(A.at[0], A.at[1], a_s, a_r, mate, z)
    swap.start()
    sent.append(swap)

    half = count // 2 if count % 2 == 0 else count
    low, top = R * size, R * size + n

    def compute(block, slot, first):
        @pl.loop(0, count // half)
        def _(c):
            rows = pl.ds(pl.multiple_of(c * half * tall, 16), half * tall)
            t = jnp.dot(A[slot, rows, :], block[0:K, :], preferred_element_type=f32)
            t = jnp.concatenate(
                [t[g * tall:(g + 1) * tall] * ws[pl.ds(c * half + g, 1), :] for g in range(half)], axis=0
            ).astype(bf16)
            o = lax.dot_general(t, block[low:top, :], (((1,), (1,)), ((), ())), preferred_element_type=f32)
            if first:
                acc[slot, rows, :] = o
            else:
                acc[slot, rows, :] += o

    back = send(rs, rr, r_s, r_r, mate, z)
    sent.append(back)
    for k in range(Z):
        if k:
            for c in blocks[k - 1][5] + [blocks[k - 1][4][0][1], blocks[k - 1][4][1][0]]:
                c.wait_recv()
            block = F.at[blocks[k - 1][0]]
        else:
            block = fin
        shape = (ws.shape[0], L - top)
        pick = lax.broadcasted_iota(jnp.int32, shape, 1) == lax.broadcasted_iota(jnp.int32, shape, 0) + z * count
        ws[...] = jnp.dot(jnp.where(pick, 1.0, 0.0).astype(bf16), block[top:L, :], preferred_element_type=f32)
        if k == 0:
            compute(block, 0, True)
            swap.wait_recv()
            compute(block, 1, True)
            if Z > 2:
                turn(Z - 1)
        else:
            compute(block, 1, False)
            if k == Z - 1:
                rs[...] = acc[1].astype(bf16)
                back.start()
            compute(block, 0, False)
    back.wait_recv()
    for i in range(count):
        rows = slice(i * tall, (i + 1) * tall)
        out[i] = (acc[0, rows, :] + rr[rows, :].astype(f32)).astype(bf16)[: out.shape[1]]
    for c in sent:
        c.wait_send()
    for there, c in firsts:
        pl.when(there)(c.wait_send)
    for block in blocks:
        for c in block[2]:
            pl.when(block[3])(c.wait_send)


def fused(R, Z, halves, first_factor, second_factor, weights):
    bf16 = jnp.bfloat16
    S, C = R // Z, R // 2
    O, a, b = halves.shape
    q, v = first_factor.shape
    n = second_factor.shape[1]
    count, step = O // Z, b // S
    tall = up(a, 16)
    K = up(R * a, 128)
    wide = up(-(-q // R), 128)
    core = lax.rem(lax.axis_index("row"), 2)
    L = up(R * a + n + O, 16)
    full = jnp.concatenate([first_factor.T, second_factor.T, weights.T], axis=0)
    full = jnp.pad(full, ((0, L - R * a - n - O), (0, R * wide - q)))
    fin = lax.dynamic_slice_in_dim(full, core * (C * wide), C * wide, 1)
    hin = halves.reshape(Z, count, a, S, step).transpose(0, 3, 2, 1, 4).reshape(R, a, count * step)
    lanes = up(count * step, 128)
    hin = jnp.pad(hin, ((0, 0), (0, tall - a), (0, lanes - count * step)))
    dma, vmem = pltpu.SemaphoreType.DMA, pltpu.VMEM
    big = pl.BlockSpec(memory_space=pltpu.VMEM)
    return pl.pallas_call(
        functools.partial(kernel, R, Z, n, wide, L),
        out_shape=jax.ShapeDtypeStruct((count, a, n), bf16),
        in_specs=[big, big],
        out_specs=big,
        scratch_shapes=[
            vmem((Z, L, C * wide), bf16),
            vmem((R, tall, lanes), bf16),
            vmem((R, tall, lanes), bf16),
            vmem((2, count * tall, K), bf16),
            vmem((2, count * tall, n), jnp.float32),
            vmem((up(count, 16), C * wide), jnp.float32),
            vmem((count * tall, n), bf16),
            vmem((count * tall, n), bf16),
            dma((2, Z, 2)), dma((2, Z, 2)),
            dma((Z - 1, 2, 2)), dma((Z - 1, 2, 2)),
            dma((Z - 1, 2)), dma((Z - 1, 2)),
            dma((Z - 1,)), dma((Z - 1,)),
            dma((R - 1,)), dma((R - 1,)),
            dma, dma, dma, dma, dma,
        ],
        compiler_params=pltpu.CompilerParams(
            collective_id=0, has_side_effects=True, vmem_limit_bytes=56 * 1024 * 1024
        ),
    )(fin, hin)


def fits(mesh):
    R, Z = mesh.shape["row"], mesh.shape["col"]
    return R % Z == 0 and R == 8 and Z > 2


def solution(mesh):
    placed = (P(None, "row", "col"), P("col", None), P("col", None), P("col", None))
    rows, cols = mesh.shape["row"], mesh.shape["col"]

    def run(*arrays):
        if fits(mesh):
            return fused(rows, cols, *arrays)
        return body(rows, *arrays)

    return jax.shard_map(
        run, mesh=mesh, in_specs=placed, out_specs=P("col", "row", None), check_vma=False
    )
```
